256 devices in a mesh: frame: 64 (over x, y_hi, z), head: 4 (over y_lo, core).
Axes of the slice: x: 4, y: 4 (y_hi: 2, y_lo: 2; y = y_hi * 2 + y_lo), z: 8, core: 2. Of those that a mesh axis runs over, the one named last changes fastest.
Arguments:
- frames: bfloat16 [32768, 1536], P('frame'), may hold values from -24 to 24
- glu_weight: bfloat16 [2, 1536, 1536], P(None, None, 'head'), may hold values from -0.15625 to 0.15625
- depth_kernel: float32 [31, 1536], P(None, 'head'), may hold values from -1 to 1
- bn_scale: float32 [1536], P('head'), may hold values from 0.5 to 2
- bn_shift: float32 [1536], P('head'), may hold values from -2.5 to 2.5
- point_weight: bfloat16 [1536, 1536], P('head'), may hold values from -0.15625 to 0.15625
- qkv_weight: bfloat16 [3, 1536, 1536], P(None, None, 'head'), may hold values from -3 to 3
- out_weight: bfloat16 [1536, 1536], P('head'), may hold values from -0.15625 to 0.15625
Outputs:
- block_out: bfloat16 [32768, 1536], P('frame', 'head')
The draws below stay inside these ranges and needn't reach their ends.
All inputs are finite; a program needn't handle non-finite values.
Results may differ from the reference program's by a relative error of at most 0.018.
Values may be sent and summed in bfloat16 or wider, within the bound.
A program may use at most 128 MiB of HBM per device.

```python
import math
import jax
import jax.numpy as jnp
from jax import lax

D = 1536
HEADS = 16
HD = 96
KW = 31
HALF = 15
ROUNDS = 4
TOK_DEV = 512
TOKENS = 32768
N_FRAME = 64


def draw_frames(key, part):
    key = jax.random.fold_in(key, 11)
    key_parts = jax.random.split(key, 3)
    row_scale = jnp.exp(jax.random.uniform(key_parts[1], (TOKENS, 1), minval=math.log(0.3), maxval=math.log(3.0)))
    column_scale = jnp.exp(jax.random.uniform(key_parts[2], (1, D), minval=math.log(0.4), maxval=math.log(2.5)))
    entries = jnp.clip(jax.random.normal(key_parts[0], (TOKENS, D)), -3.0, 3.0)
    result = entries * row_scale * column_scale
    return result.astype(jnp.bfloat16)


def draw_qkv_weight(key, part):
    key = jax.random.fold_in(key, 23)
    key_parts = jax.random.split(key, 1)
    entries = jnp.clip(jax.random.normal(key_parts[0], (3, D, D)), -4.0, 4.0)
    spread = jnp.array([math.sqrt(2.0), math.sqrt(2.0), 3.0], jnp.float32)
    entries = entries * spread[:, None, None] * D ** (-0.5)
    return jnp.clip(entries, -3.0, 3.0).astype(jnp.bfloat16)


def level_of(rng, dims, pieces, smallest, high):
    level = 1.0
    for dim, parts in pieces:
        draws = jax.random.uniform(jax.random.fold_in(jax.random.fold_in(rng, 6), dim), (parts,), jnp.float32, smallest / len(pieces), high / len(pieces))
        level = level * jnp.repeat(jnp.exp(draws), dims[dim] // parts).reshape((-1,) + (1,) * (len(dims) - 1 - dim))
    return level


def gaussian(own_key, shape, scale, limit, shards=(), kind=jnp.bfloat16):
    drawn = scale * jax.random.normal(own_key, shape, jnp.float32)
    if shards:
        drawn = drawn * level_of(own_key, shape, shards, -0.22, 0.18)
    return jnp.clip(drawn, -limit, limit).astype(kind)


def setup_inputs(seed: int = 0) -> dict:
    key_list = jax.random.split(jax.random.key(seed), 9)
    frames = draw_frames(jax.random.fold_in(key_list[8], 71), 0)
    glu_weight = gaussian(key_list[1], (2, D, D), D ** -0.5, 0.15625, ((2, 4),))
    depth_kernel = gaussian(key_list[2], (KW, D), KW ** -0.5, 1.0, ((1, 4),), jnp.float32)
    bn_scale = jnp.clip(jnp.exp(math.log(2.0) - 1.3862944 * jax.random.uniform(key_list[3], (D,), jnp.float32) ** level_of(key_list[3], (D,), ((0, 4),), -0.2, 0.2)), 0.5, 2.0)
    bn_shift = gaussian(key_list[4], (D,), 0.5, 2.5, ((0, 4),), jnp.float32)
    point_weight = gaussian(key_list[5], (D, D), D ** -0.5, 0.15625, ((0, 4),))
    qkv_weight = draw_qkv_weight(jax.random.fold_in(key_list[8], 71), 0)
    out_weight = gaussian(key_list[7], (D, D), D ** -0.5, 0.15625, ((0, 4),))
    return {"frames": frames, "glu_weight": glu_weight, "depth_kernel": depth_kernel, "bn_scale": bn_scale, "bn_shift": bn_shift, "point_weight": point_weight, "qkv_weight": qkv_weight, "out_weight": out_weight}


def layer_norm(inputs):
    center = inputs - lax.optimization_barrier(jnp.mean(inputs, axis=-1, keepdims=True))
    spread = lax.optimization_barrier(jnp.mean(center * center, axis=-1, keepdims=True))
    return center * lax.rsqrt(spread + 1e-05)

def rotary(inputs, positions):
    half_size = HD // 2
    exponent = jnp.arange(half_size, dtype=jnp.float32) * (2.0 / HD)
    inverse = jnp.power(jnp.float32(10000.0), -exponent)
    angles = positions[:, None] * inverse[None, :]
    cosine = jnp.cos(angles)[:, None, :]
    sine_part = jnp.sin(angles)[:, None, :]
    shaped = inputs.reshape(inputs.shape[0], -1, HD)
    first_half = shaped[..., :half_size]
    second_half = shaped[..., half_size:]
    turned = jnp.concatenate([first_half * cosine - second_half * sine_part, second_half * cosine + first_half * sine_part], axis=-1)
    return turned.reshape(inputs.shape)

def reference(frames, glu_weight, depth_kernel, bn_scale, bn_shift, point_weight, qkv_weight, out_weight):
    frames_wide = frames.astype(jnp.float32)
    normed = layer_norm(frames_wide).astype(jnp.bfloat16)
    value_part = jnp.dot(normed, glu_weight[0], preferred_element_type=jnp.float32)
    gate_part = jnp.dot(normed, glu_weight[1], preferred_element_type=jnp.float32)
    gated_units = (value_part * jax.nn.sigmoid(gate_part)).astype(jnp.bfloat16)
    padded = jnp.pad(gated_units.astype(jnp.float32), ((HALF, HALF), (0, 0)))
    convolved = jnp.zeros((TOKENS, D), jnp.float32)
    for tap_index in range(KW):
        convolved = convolved + padded[tap_index:tap_index + TOKENS] * depth_kernel[tap_index]
    shifted = convolved * bn_scale + bn_shift
    swished = (shifted * jax.nn.sigmoid(shifted)).astype(jnp.bfloat16)
    residual = frames_wide + jnp.dot(swished, point_weight, preferred_element_type=jnp.float32)
    normed_again = layer_norm(residual).astype(jnp.bfloat16)
    positions = jnp.arange(TOKENS, dtype=jnp.float32)
    queries = rotary(jnp.dot(normed_again, qkv_weight[0], preferred_element_type=jnp.float32), positions).astype(jnp.bfloat16)
    keys_all = rotary(jnp.dot(normed_again, qkv_weight[1], preferred_element_type=jnp.float32), positions).astype(jnp.bfloat16)
    values_all = jnp.dot(normed_again, qkv_weight[2], preferred_element_type=jnp.float32).astype(jnp.bfloat16)
    query_blocks = queries.reshape(N_FRAME, TOK_DEV, HEADS, HD)
    key_blocks = keys_all.reshape(N_FRAME, TOK_DEV, HEADS, HD)
    value_blocks = values_all.reshape(N_FRAME, TOK_DEV, HEADS, HD)
    offsets = jnp.arange(-ROUNDS, ROUNDS + 1, dtype=jnp.int32)
    score_scale = HD ** (-0.5)

    def one_block(carry_in):
        block_index, query_block = carry_in
        chosen = ((block_index + offsets) % N_FRAME).astype(jnp.int32)
        keys_near = key_blocks[chosen].reshape(-1, HEADS, HD).astype(jnp.float32)
        values_near = value_blocks[chosen].reshape(-1, HEADS, HD).astype(jnp.float32)
        scores = jnp.einsum('qhd,khd->hqk', query_block.astype(jnp.float32), keys_near) * score_scale
        largest = lax.optimization_barrier(jnp.max(scores, axis=-1, keepdims=True))
        weights = jnp.exp(scores - largest)
        totals = lax.optimization_barrier(jnp.sum(weights, axis=-1))
        rounded = lax.optimization_barrier(weights.astype(jnp.bfloat16)).astype(jnp.float32)
        mixture = jnp.einsum('hqk,khd->qhd', rounded, values_near)
        return mixture / totals.T[:, :, None]
    attended = lax.map(one_block, (jnp.arange(N_FRAME, dtype=jnp.int32), query_blocks))
    attended = attended.reshape(TOKENS, D).astype(jnp.bfloat16)
    return (residual + jnp.dot(attended, out_weight, preferred_element_type=jnp.float32)).astype(jnp.bfloat16)
```

```python
import functools

import jax
import jax.numpy as jnp
import numpy as np
from jax import lax
from jax.experimental import pallas as pl
from jax.experimental.pallas import tpu as pltpu
from jax.sharding import PartitionSpec as P

D = 1536
HD = 96
HALF_HD = HD // 2
KW = 31
HALF = 15
EDGE = 16
ROWS = 512
WIDTH = 384
QUARTER = 96
PIECE = 48
PART = 128
PARTS = ROWS // PART
SHARE = PART // 2
LANES = 128
CHUNK = 128
CHUNKS = ROWS // CHUNK
HEADS_HERE = 4
RING = 8
GROUP = 4
WINDOW = 9
UNIT = 2 * HD
PADDED_UNIT = UNIT + 16
SCALE = HD ** (-0.5) * 1.4426950408889634
MESH = pl.DeviceIdType.MESH
F32 = jnp.float32
BF16 = jnp.bfloat16


def contract(lhs, rhs, lhs_dim, rhs_dim):
    return lax.dot_general(
        lhs, rhs, (((lhs_dim,), (rhs_dim,)), ((), ())), preferred_element_type=F32
    )


def place(frame_count):
    frame = lax.axis_index("frame")
    head = lax.axis_index("head")
    ring, spot = frame // RING, frame % RING
    half, slot = spot // GROUP, spot % GROUP
    pair, core = head // 2, head % 2
    groups = frame_count // GROUP

    def partner(index):
        return (RING * ring + GROUP * core + index, 2 * pair + half)

    def is_self(index):
        return jnp.logical_and(core == half, slot == index)

    def group_device(by):
        group = (2 * ring + core + by + groups) % groups
        return (RING * (group // 2) + spot, 2 * pair + group % 2)

    def head_device(pair_flip, core_flip):
        to_pair = 1 - pair if pair_flip else pair
        to_core = 1 - core if core_flip else core
        return (frame, 2 * to_pair + to_core)

    def frame_device(by):
        return ((frame + by + frame_count) % frame_count, head)

    def spot_device(by):
        return (RING * ring + (spot + by + RING) % RING, head)

    def other_device():
        return (2 * RING * (ring // 2) + RING * (1 - ring % 2) + spot, 2 * (1 - pair) + core)

    return (
        partner,
        is_self,
        group_device,
        head_device,
        frame_device,
        spot_device,
        other_device,
        half,
        slot,
        core,
    )


def remote(source, target, send_sem, recv_sem, device):
    return pltpu.make_async_remote_copy(
        src_ref=source,
        dst_ref=target,
        send_sem=send_sem,
        recv_sem=recv_sem,
        device_id=device,
        device_id_type=MESH,
    )


def norm_rows(block):
    wide = block.astype(F32)
    center = wide - jnp.mean(wide, axis=-1, keepdims=True)
    spread = jnp.mean(center * center, axis=-1, keepdims=True)
    return (center * lax.rsqrt(spread + 1e-05)).astype(BF16)


def kernel(
    frame_count,
    frames_hbm,
    glu_hbm,
    depth_hbm,
    scale_hbm,
    shift_hbm,
    point_hbm,
    qkv_hbm,
    weight_hbm,
    angle_hbm,
    out_ref,
    frames,
    glu,
    point_all,
    key_value_weight,
    query_weight,
    weight_ref,
    angle,
    taps_ref,
    scale_ref,
    shift_ref,
    edges,
    normed,
    gated,
    swished,
    swished_all,
    sums,
    terms,
    residual,
    residual_send,
    normed_again,
    rotation,
    kv_ref,
    q_ref,
    kv_all,
    keys,
    q_all,
    scores,
    far_scores,
    peaks,
    totals,
    mixed,
    gathered,
    near_send,
    near_recv,
    far_own,
    far_send,
    far_recv,
    load_sem,
    edge_send_sem,
    edge_recv_sem,
    weight_y_send_sem,
    weight_y_recv_sem,
    weight_x_send_sem,
    weight_x_recv_sem,
    weight_near_send_sem,
    weight_near_recv_sem,
    swished_send_sem,
    swished_recv_sem,
    normed_send_sem,
    normed_recv_sem,
    residual_send_sem,
    residual_recv_sem,
    kv_send_sem,
    kv_recv_sem,
    q_send_sem,
    q_recv_sem,
    relay_send_sem,
    relay_recv_sem,
    o_send_sem,
    o_recv_sem,
    near_send_sem,
    near_recv_sem,
    far_send_sem,
    far_recv_sem,
):
    (
        partner,
        is_self,
        group_device,
        head_device,
        frame_device,
        spot_device,
        other_device,
        half,
        slot,
        core,
    ) = place(frame_count)
    frame = lax.axis_index("frame")
    own_head = lax.axis_index("head")
    pair = own_head // 2
    near_head = 2 * pair + 1 - core
    far_head = 2 * (1 - pair) + core
    cross_head = 2 * (1 - pair) + 1 - core

    def columns_of(head):
        return pl.ds(pl.multiple_of(head * WIDTH, 128), WIDTH)

    colour = (frame // (2 * RING) + frame % RING) % 4
    quarters = [colour, (colour + 2) % 4, (colour + 3) % 4, (colour + 1) % 4]

    def point_rows(head, start, size):
        return point_all.at[pl.ds(pl.multiple_of(head * WIDTH + start, 16), size)]

    loads = [
        pltpu.make_async_copy(point_hbm, point_rows(own_head, 0, WIDTH), load_sem.at[0]),
        pltpu.make_async_copy(frames_hbm, frames, load_sem.at[1]),
        pltpu.make_async_copy(glu_hbm.at[0], glu.at[:, pl.ds(0, WIDTH)], load_sem.at[2]),
        pltpu.make_async_copy(glu_hbm.at[1], glu.at[:, pl.ds(WIDTH, WIDTH)], load_sem.at[3]),
        pltpu.make_async_copy(depth_hbm, taps_ref, load_sem.at[4]),
        pltpu.make_async_copy(scale_hbm, scale_ref.at[0], load_sem.at[5]),
        pltpu.make_async_copy(shift_hbm, shift_ref.at[0], load_sem.at[6]),
        pltpu.make_async_copy(angle_hbm, angle, load_sem.at[7]),
        pltpu.make_async_copy(
            qkv_hbm.at[1], key_value_weight.at[:, pl.ds(0, WIDTH)], load_sem.at[8]
        ),
        pltpu.make_async_copy(
            qkv_hbm.at[2], key_value_weight.at[:, pl.ds(WIDTH, WIDTH)], load_sem.at[9]
        ),
        pltpu.make_async_copy(qkv_hbm.at[0], query_weight, load_sem.at[10]),
        pltpu.make_async_copy(weight_hbm, weight_ref, load_sem.at[11]),
    ]
    for load in loads[:7]:
        load.start()

    barrier = pltpu.get_barrier_semaphore()

    def greet(device):
        pl.semaphore_signal(barrier, inc=1, device_id=device, device_id_type=MESH)

    for index in range(GROUP):

        @pl.when(jnp.logical_not(is_self(index)))
        def _():
            greet(partner(index))

    greet(group_device(1))
    greet(group_device(-1))
    greet(head_device(False, True))
    greet(head_device(True, False))
    greet(head_device(True, True))
    greet(frame_device(1))
    greet(frame_device(-1))
    greet(frame_device(2 * RING))
    greet(frame_device(-2 * RING))
    greet(other_device())
    greet(spot_device(1))
    greet(spot_device(-1))
    pl.semaphore_wait(barrier, 16 - (core == half).astype(jnp.int32))

    def weight_y_copy(turn, side):
        block = point_rows(own_head, QUARTER * quarters[turn] + PIECE * side, PIECE)
        return remote(
            block,
            block,
            weight_y_send_sem.at[turn, side],
            weight_y_recv_sem.at[turn, side],
            other_device() if side else head_device(True, False),
        )

    def weight_y_arrival(turn, side):
        block = point_rows(far_head, QUARTER * quarters[turn] + PIECE * side, PIECE)
        return remote(
            block,
            block,
            weight_y_send_sem.at[turn, side],
            weight_y_recv_sem.at[turn, side],
            other_device() if side else head_device(True, False),
        )

    def weight_x_copy(way, side):
        block = point_rows(far_head, QUARTER * quarters[0] + PIECE * side, PIECE)
        return remote(
            block,
            block,
            weight_x_send_sem.at[way, side],
            weight_x_recv_sem.at[way, side],
            spot_device(-1 if way else 1) if side else frame_device(-2 * RING if way else 2 * RING),
        )

    def weight_x_arrival(way, side):
        block = point_rows(far_head, QUARTER * quarters[2 + way] + PIECE * side, PIECE)
        return remote(
            block,
            block,
            weight_x_send_sem.at[way, side],
            weight_x_recv_sem.at[way, side],
            spot_device(-1 if way else 1) if side else frame_device(-2 * RING if way else 2 * RING),
        )

    def weight_near_copy(index, arriving):
        if index == 0:
            block = point_rows(near_head if arriving else own_head, 0, WIDTH)
        else:
            block = point_rows(
                cross_head if arriving else far_head, QUARTER * quarters[index - 1], QUARTER
            )
        return remote(
            block,
            block,
            weight_near_send_sem.at[index],
            weight_near_recv_sem.at[index],
            head_device(False, True),
        )

    loads[0].wait()
    weight_y_copy(0, 0).start()
    weight_y_copy(0, 1).start()
    loads[1].wait()

    def edge_copy(side):
        rows = pl.ds(ROWS - EDGE, EDGE) if side == 0 else pl.ds(0, EDGE)
        return remote(
            frames.at[rows],
            edges.at[side],
            edge_send_sem.at[side],
            edge_recv_sem.at[side],
            frame_device(1 if side == 0 else -1),
        )

    edge_copy(0).start()
    edge_copy(1).start()

    def norm_block(index, carry):
        start = pl.multiple_of(index * 64, 64)
        normed[pl.ds(pl.multiple_of(start + EDGE, 16), 64)] = norm_rows(frames[pl.ds(start, 64)])
        return carry

    lax.fori_loop(0, ROWS // 64, norm_block, 0)
    weight_y_copy(1, 0).start()
    weight_y_copy(1, 1).start()
    weight_near_copy(0, False).start()
    for load in loads[7:]:
        load.start()
    edge_copy(0).wait_recv()
    normed[:EDGE] = norm_rows(edges[0])
    edge_copy(1).wait_recv()
    normed[ROWS + EDGE :] = norm_rows(edges[1])

    loads[2].wait()
    loads[3].wait()
    both = jnp.dot(normed[...], glu[...], preferred_element_type=F32)
    gated[...] = (both[:, :WIDTH] * jax.nn.sigmoid(both[:, WIDTH:])).astype(BF16).astype(F32)

    for side in range(2):
        weight_y_arrival(0, side).wait_recv()
        weight_x_copy(0, side).start()
        weight_x_copy(1, side).start()
    weight_near_copy(1, False).start()

    @pl.when(frame == 0)
    def _():
        gated[:EDGE] = jnp.zeros((EDGE, WIDTH), F32)

    @pl.when(frame == frame_count - 1)
    def _():
        gated[ROWS + EDGE :] = jnp.zeros((EDGE, WIDTH), F32)

    for load in loads[4:7]:
        load.wait()

    def share_rows(part, which):
        return pl.ds(pl.multiple_of(part * PART + SHARE * which, SHARE), SHARE)

    def swished_copy(part, index):
        flips = ((False, True), (True, False), (True, True))[index]
        return remote(
            swished.at[share_rows(part, core if index == 1 else 1 - core)],
            swished_all.at[part, own_head],
            swished_send_sem.at[part, index],
            swished_recv_sem.at[part, index],
            head_device(*flips),
        )

    def swished_arrival(part, index):
        head = (near_head, far_head, cross_head)[index]
        return remote(
            swished.at[share_rows(part, core)],
            swished_all.at[part, head],
            swished_send_sem.at[part, index],
            swished_recv_sem.at[part, index],
            head_device(False, True),
        )

    def normed_copy(part, arriving):
        block = normed_again.at[share_rows(part, 1 - core if arriving else core)]
        return remote(
            block,
            block,
            normed_send_sem.at[part],
            normed_recv_sem.at[part],
            head_device(False, True),
        )

    def residual_copy(part, arriving):
        return remote(
            residual_send.at[part],
            residual.at[share_rows(part, 1 - core if arriving else core)],
            residual_send_sem.at[part],
            residual_recv_sem.at[part],
            head_device(False, True),
        )

    def convolve(part):
        def piece(index, carry):
            lanes = pl.ds(pl.multiple_of(index * LANES, LANES), LANES)
            start = part * PART
            block = gated[pl.ds(start, PART + 2 * EDGE), lanes]
            taps = taps_ref[:, lanes]
            total = jnp.zeros((PART, LANES), F32)
            for shift in range(8):
                partial = jnp.zeros((PART + 8, LANES), F32)
                for step in range(4):
                    tap = 8 * step + shift - 1
                    if 0 <= tap < KW:
                        partial += taps[tap : tap + 1] * block[8 * step : 8 * step + PART + 8]
                total += partial[shift : shift + PART]
            shifted = total * scale_ref[:, lanes] + shift_ref[:, lanes]
            swished[pl.ds(start, PART), lanes] = (shifted * jax.nn.sigmoid(shifted)).astype(BF16)
            return carry

        lax.fori_loop(0, WIDTH // LANES, piece, 0)
        for index in (1, 2, 0):
            swished_copy(part, index).start()
        swished_all[part, own_head] = swished[share_rows(part, core)]

    def add_residual(part):
        for index in range(3):
            swished_arrival(part, index).wait_recv()
        rows = share_rows(part, core)
        whole = jnp.concatenate([swished_all[part, head] for head in range(4)], axis=1)
        sums[...] = frames[rows].astype(F32) + jnp.dot(
            whole, point_all[...], preferred_element_type=F32
        )
        normed_again[rows] = norm_rows(sums[...])
        normed_copy(part, False).start()
        residual[rows] = sums[:, columns_of(own_head)]
        residual_send[part] = sums[:, columns_of(near_head)]
        residual_copy(part, False).start()

    def kv_copy(part, index):
        return remote(
            kv_ref.at[part, index],
            kv_all.at[GROUP + slot, part, pl.ds(0, UNIT)],
            kv_send_sem.at[part, index],
            kv_recv_sem.at[part, slot],
            partner(index),
        )

    def kv_arrival(part, index):
        return remote(
            kv_ref.at[part, index],
            kv_all.at[GROUP + index, part, pl.ds(0, UNIT)],
            kv_send_sem.at[part, index],
            kv_recv_sem.at[part, index],
            partner(index),
        )

    def project(part):
        normed_copy(part, True).wait_recv()
        columns = pl.ds(part * PART, PART)
        turned = jnp.dot(
            normed_again[pl.ds(part * PART, PART)],
            key_value_weight[...],
            preferred_element_type=F32,
        ).T
        cosine, sine = rotation[0, :, columns], rotation[1, :, columns]
        for index in range(HEADS_HERE):
            base = index * HD
            first = turned[base : base + HALF_HD]
            second = turned[base + HALF_HD : base + HD]
            kv_ref[part, index, :HALF_HD] = (first * cosine - second * sine).astype(BF16)
            kv_ref[part, index, HALF_HD:HD] = (second * cosine + first * sine).astype(BF16)
            kv_ref[part, index, HD:] = turned[WIDTH + base : WIDTH + base + HD].astype(BF16)

    def send_pairs(part):
        for index in range(GROUP):

            @pl.when(jnp.logical_not(is_self(index)))
            def _():
                kv_copy(part, index).start()

            @pl.when(is_self(index))
            def _():
                kv_all[GROUP + slot, part, :UNIT] = kv_ref[part, index]

    def await_sent(copy, part):
        for index in range(GROUP):

            @pl.when(jnp.logical_not(is_self(index)))
            def _():
                copy(part, index).wait_send()

    for part in range(PARTS):
        convolve(part)

    for side in range(2):
        weight_y_arrival(1, side).wait_recv()
    weight_near_copy(2, False).start()
    for way in range(2):
        for side in range(2):
            weight_x_arrival(way, side).wait_recv()
        weight_near_copy(3 + way, False).start()

    loads[7].wait()
    lane = lax.broadcasted_iota(jnp.int32, (2, HALF_HD, LANES), 2)
    far = jnp.sum(
        jnp.where(lane == frame, angle[:, :, ROWS:], 0.0), axis=-1, keepdims=True
    )
    cosine, sine = angle[0, :, :ROWS], angle[1, :, :ROWS]
    rotation[0] = cosine * far[0] - sine * far[1]
    rotation[1] = sine * far[0] + cosine * far[1]
    for block in range(3 * GROUP):
        kv_all[block, :, UNIT:] = jnp.ones((PARTS, PADDED_UNIT - UNIT, PART), BF16)
    for load in loads[8:]:
        load.wait()

    for index in range(5):
        weight_near_copy(index, True).wait_recv()
    add_residual(0)
    for part in range(1, PARTS):
        add_residual(part)
        project(part - 1)
        if part <= 2:
            send_pairs(part - 1)
    project(PARTS - 1)

    turned_queries = (
        jnp.dot(normed_again[...], query_weight[...], preferred_element_type=F32) * SCALE
    ).T
    for index in range(HEADS_HERE):
        base = index * HD
        first = turned_queries[base : base + HALF_HD]
        second = turned_queries[base + HALF_HD : base + HD]
        cosine, sine = rotation[0], rotation[1]
        low = (first * cosine - second * sine).astype(BF16)
        high = (second * cosine + first * sine).astype(BF16)
        for chunk in range(CHUNKS):
            columns = slice(chunk * CHUNK, (chunk + 1) * CHUNK)
            q_ref[chunk, index, :HALF_HD] = low[:, columns]
            q_ref[chunk, index, HALF_HD:] = high[:, columns]

    def q_copy(chunk, index):
        return remote(
            q_ref.at[chunk, index],
            q_all.at[chunk, slot],
            q_send_sem.at[chunk, index],
            q_recv_sem.at[chunk, slot],
            partner(index),
        )

    def send_queries(chunk):
        for index in range(GROUP):

            @pl.when(jnp.logical_not(is_self(index)))
            def _():
                q_copy(chunk, index).start()

            @pl.when(is_self(index))
            def _():
                q_all[chunk, slot] = q_ref[chunk, index]

    def turn_keys(block, part):
        keys[block, pl.ds(part * PART, PART)] = kv_all[block, part, :HD].T

    def relay(part, index, upward):
        at = index if upward else 2 * GROUP + index
        flag = index if upward else GROUP + index
        return remote(
            kv_all.at[GROUP + index, part, pl.ds(0, UNIT)],
            kv_all.at[at, part, pl.ds(0, UNIT)],
            relay_send_sem.at[part, flag],
            relay_recv_sem.at[part, flag],
            group_device(1 if upward else -1),
        )

    for part in range(PARTS):
        await_sent(kv_copy, part)
        if part + 2 < PARTS:
            send_pairs(part + 2)
        else:
            send_queries(part + 2 - PARTS)
        for index in range(GROUP):

            @pl.when(jnp.logical_not(is_self(index)))
            def _():
                kv_arrival(part, index).wait_recv()

            relay(part, index, True).start()
            relay(part, index, False).start()
            turn_keys(GROUP + index, part)

    def relay_arrivals(near):
        low = core == (1 if near else 0)
        for part in range(PARTS):
            for index in range(GROUP):
                at = jnp.where(low, index, 2 * GROUP + index)
                flag = jnp.where(low, index, GROUP + index)
                remote(
                    kv_all.at[GROUP + index, part, pl.ds(0, UNIT)],
                    kv_all.at[at, part, pl.ds(0, UNIT)],
                    relay_send_sem.at[part, flag],
                    relay_recv_sem.at[part, flag],
                    group_device(1),
                ).wait_recv()
                turn_keys(at, part)

    relay_arrivals(True)

    def await_queries(chunk):
        for index in range(GROUP):

            @pl.when(jnp.logical_not(is_self(index)))
            def _():
                remote(
                    q_ref.at[chunk, index],
                    q_all.at[chunk, index],
                    q_send_sem.at[chunk, index],
                    q_recv_sem.at[chunk, index],
                    partner(index),
                ).wait_recv()

    def query_block(turn):
        return jnp.where(core == 1, turn, GROUP - 1 - turn)

    def key_block(turn, index):
        return jnp.where(core == 1, turn + index, 3 * GROUP - 1 - turn - index)

    def score(chunk, turn, first, last, target, buffer):
        turned = q_all[chunk, query_block(turn)]
        for index in range(first, last):
            target[buffer, index - first] = contract(
                keys[key_block(turn, index)], turned, 1, 0
            )

    def weigh(turn, first, last, source, buffer, largest, total):
        for index in range(first, last):
            weights = jnp.exp2(source[buffer, index - first] - largest).astype(BF16)
            block = key_block(turn, index)
            values = jnp.concatenate(
                [kv_all[block, part, HD:] for part in range(PARTS)], axis=1
            )
            total += contract(values, weights, 1, 0)
        return total

    def highest(source, buffer, count):
        return functools.reduce(
            jnp.maximum,
            [jnp.max(source[buffer, index], axis=0, keepdims=True) for index in range(count)],
        )

    def near_turn(chunk, turn, buffer):
        count = WINDOW - 1 - turn
        largest = highest(scores, buffer, count)
        peaks[chunk, turn, 0:1] = largest
        totals[chunk, turn] = weigh(
            turn, 0, count, scores, buffer, largest, jnp.zeros((HD + 16, CHUNK), F32)
        )

    def near_stage(chunk):
        score(chunk, 0, 0, WINDOW - 1, scores, 0)
        for turn in range(GROUP):
            if turn < GROUP - 1:
                score(chunk, turn + 1, 0, WINDOW - 2 - turn, scores, (turn + 1) % 2)
            near_turn(chunk, turn, turn % 2)

    def far_turn(chunk, turn, buffer):
        earlier = peaks[chunk, turn, 0:1]
        largest = jnp.maximum(earlier, highest(far_scores, buffer, turn + 1))
        total = weigh(
            turn,
            WINDOW - 1 - turn,
            WINDOW,
            far_scores,
            buffer,
            largest,
            totals[chunk, turn] * jnp.exp2(earlier - largest),
        )
        mixed[chunk, turn] = (total[:HD] / total[HD : HD + 1]).astype(BF16)

    def far_stage(chunk):
        score(chunk, 0, WINDOW - 1, WINDOW, far_scores, 0)
        for turn in range(GROUP):
            if turn < GROUP - 1:
                score(chunk, turn + 1, WINDOW - 2 - turn, WINDOW, far_scores, (turn + 1) % 2)
            far_turn(chunk, turn, turn % 2)

    def o_copy(chunk, turn):
        return remote(
            mixed.at[chunk, turn],
            gathered.at[chunk, slot],
            o_send_sem.at[chunk, turn],
            o_recv_sem.at[chunk, slot],
            partner(query_block(turn)),
        )

    def send_mixed(chunk):
        for turn in range(GROUP):

            @pl.when(is_self(query_block(turn)))
            def _():
                gathered[chunk, slot] = mixed[chunk, turn]

            @pl.when(jnp.logical_not(is_self(query_block(turn))))
            def _():
                o_copy(chunk, turn).start()

    def near_copy(chunk):
        return remote(
            near_send.at[chunk],
            near_recv.at[chunk],
            near_send_sem.at[chunk],
            near_recv_sem.at[chunk],
            head_device(False, True),
        )

    def far_copy(chunk):
        return remote(
            far_send.at[chunk],
            far_recv.at[chunk],
            far_send_sem.at[chunk],
            far_recv_sem.at[chunk],
            head_device(True, False),
        )

    def rows_of(chunk):
        return pl.ds(pl.multiple_of(chunk * CHUNK, CHUNK), CHUNK)

    def project_out(chunk):
        for index in range(GROUP):

            @pl.when(jnp.logical_not(is_self(index)))
            def _():
                remote(
                    mixed.at[chunk, index],
                    gathered.at[chunk, index],
                    o_send_sem.at[chunk, index],
                    o_recv_sem.at[chunk, index],
                    partner(index),
                ).wait_recv()

        turned = gathered[chunk].reshape(WIDTH, CHUNK).T
        terms[...] = jnp.dot(turned, weight_ref[...], preferred_element_type=F32)
        near_send[chunk, 0] = terms[:, columns_of(near_head)].astype(BF16)
        near_send[chunk, 1] = terms[:, columns_of(cross_head)].astype(BF16)
        near_copy(chunk).start()
        residual[rows_of(chunk)] += terms[:, columns_of(own_head)]
        far_own[chunk] = terms[:, columns_of(far_head)]

    def sum_out(chunk):
        near_copy(chunk).wait_recv()
        far_send[chunk] = (far_own[chunk] + near_recv[chunk, 1].astype(F32)).astype(BF16)
        far_copy(chunk).start()
        residual[rows_of(chunk)] += near_recv[chunk, 0].astype(F32)

    for part in range(PARTS):
        residual_copy(part, True).wait_recv()
    def early(chunk, carry):
        await_sent(q_copy, chunk)
        send_queries(chunk + 2)
        await_queries(chunk)
        near_stage(chunk)
        return carry

    lax.fori_loop(0, 2, early, 0)
    relay_arrivals(False)

    def finish(chunk, carry):
        far_stage(chunk)
        send_mixed(chunk)
        return carry

    lax.fori_loop(0, 2, finish, 0)

    def late(chunk, carry):
        await_queries(chunk)
        near_stage(chunk)
        project_out(chunk - 2)
        far_stage(chunk)
        send_mixed(chunk)
        sum_out(chunk - 2)
        return carry

    lax.fori_loop(2, CHUNKS, late, 0)
    for chunk in range(2, CHUNKS):
        project_out(chunk)
        sum_out(chunk)
    for chunk in range(CHUNKS):
        far_copy(chunk).wait_recv()
        rows = pl.ds(chunk * CHUNK, CHUNK)
        out_ref[rows] = (residual[rows] + far_recv[chunk].astype(F32)).astype(BF16)

    for index in range(GROUP):

        @pl.when(jnp.logical_not(is_self(index)))
        def _():
            for chunk in range(2, CHUNKS):
                q_copy(chunk, index).wait_send()

        for part in range(PARTS):
            relay(part, index, True).wait_send()
            relay(part, index, False).wait_send()
    for turn in range(GROUP):

        @pl.when(jnp.logical_not(is_self(query_block(turn))))
        def _():
            for chunk in range(CHUNKS):
                o_copy(chunk, turn).wait_send()

    edge_copy(0).wait_send()
    edge_copy(1).wait_send()
    for part in range(PARTS):
        normed_copy(part, False).wait_send()
        residual_copy(part, False).wait_send()
        for index in range(3):
            swished_copy(part, index).wait_send()
    for side in range(2):
        for turn in range(2):
            weight_y_copy(turn, side).wait_send()
            weight_x_copy(turn, side).wait_send()
    for index in range(5):
        weight_near_copy(index, False).wait_send()
    for chunk in range(CHUNKS):
        near_copy(chunk).wait_send()
        far_copy(chunk).wait_send()


def angle_table(frame_count):
    inverse = 10000.0 ** (-np.arange(HALF_HD) * (2.0 / HD))
    starts = np.zeros(LANES)
    starts[:frame_count] = np.arange(frame_count) * float(ROWS)
    angles = inverse[:, None] * np.concatenate([np.arange(ROWS), starts])[None, :]
    return jnp.asarray(np.stack([np.cos(angles), np.sin(angles)]).astype(np.float32))


def shards(
    frame_count,
    frames,
    glu_weight,
    depth_kernel,
    bn_scale,
    bn_shift,
    point_weight,
    qkv_weight,
    out_weight,
):
    vmem = pl.BlockSpec(memory_space=pltpu.VMEM)
    hbm = pl.BlockSpec(memory_space=pl.ANY)
    dma = pltpu.SemaphoreType.DMA
    space = pltpu.VMEM
    return pl.pallas_call(
        functools.partial(kernel, frame_count),
        out_shape=jax.ShapeDtypeStruct((ROWS, WIDTH), BF16),
        in_specs=[hbm] * 9,
        out_specs=vmem,
        scratch_shapes=[
            space((ROWS, D), BF16),
            space((D, 2 * WIDTH), BF16),
            space((D, D), BF16),
            space((D, 2 * WIDTH), BF16),
            space((D, WIDTH), BF16),
            space((WIDTH, D), BF16),
            space((2, HALF_HD, ROWS + LANES), F32),
            space((KW, WIDTH), F32),
            space((1, WIDTH), F32),
            space((1, WIDTH), F32),
            space((2, EDGE, D), BF16),
            space((ROWS + 2 * EDGE, D), BF16),
            space((ROWS + 2 * EDGE, WIDTH), F32),
            space((ROWS, WIDTH), BF16),
            space((PARTS, 4, SHARE, WIDTH), BF16),
            space((SHARE, D), F32),
            space((CHUNK, D), F32),
            space((ROWS, WIDTH), F32),
            space((PARTS, SHARE, WIDTH), F32),
            space((ROWS, D), BF16),
            space((2, HALF_HD, ROWS), F32),
            space((PARTS, GROUP, UNIT, PART), BF16),
            space((CHUNKS, GROUP, HD, CHUNK), BF16),
            space((3 * GROUP, PARTS, PADDED_UNIT, PART), BF16),
            space((3 * GROUP, ROWS, HD), BF16),
            space((CHUNKS, GROUP, HD, CHUNK), BF16),
            space((2, WINDOW - 1, ROWS, CHUNK), F32),
            space((2, GROUP, ROWS, CHUNK), F32),
            space((CHUNKS, GROUP, 8, CHUNK), F32),
            space((CHUNKS, GROUP, HD + 16, CHUNK), F32),
            space((CHUNKS, GROUP, HD, CHUNK), BF16),
            space((CHUNKS, GROUP, HD, CHUNK), BF16),
            space((CHUNKS, 2, CHUNK, WIDTH), BF16),
            space((CHUNKS, 2, CHUNK, WIDTH), BF16),
            space((CHUNKS, CHUNK, WIDTH), F32),
            space((CHUNKS, CHUNK, WIDTH), BF16),
            space((CHUNKS, CHUNK, WIDTH), BF16),
            dma((12,)),
            dma((2,)),
            dma((2,)),
            dma((2, 2)),
            dma((2, 2)),
            dma((2, 2)),
            dma((2, 2)),
            dma((5,)),
            dma((5,)),
            dma((PARTS, 3)),
            dma((PARTS, 3)),
            dma((PARTS,)),
            dma((PARTS,)),
            dma((PARTS,)),
            dma((PARTS,)),
            dma((PARTS, GROUP)),
            dma((PARTS, GROUP)),
            dma((CHUNKS, GROUP)),
            dma((CHUNKS, GROUP)),
            dma((PARTS, 2 * GROUP)),
            dma((PARTS, 2 * GROUP)),
            dma((CHUNKS, GROUP)),
            dma((CHUNKS, GROUP)),
            dma((CHUNKS,)),
            dma((CHUNKS,)),
            dma((CHUNKS,)),
            dma((CHUNKS,)),
        ],
        compiler_params=pltpu.CompilerParams(
            collective_id=1, has_side_effects=True, vmem_limit_bytes=60 << 20
        ),
    )(
        frames,
        glu_weight,
        depth_kernel,
        bn_scale,
        bn_shift,
        point_weight,
        qkv_weight,
        out_weight,
        angle_table(frame_count),
    )


def solution(mesh):
    return jax.shard_map(
        functools.partial(shards, mesh.shape["frame"]),
        mesh=mesh,
        in_specs=(
            P("frame", None),
            P(None, None, "head"),
            P(None, "head"),
            P("head"),
            P("head"),
            P("head", None),
            P(None, None, "head"),
            P("head", None),
        ),
        out_specs=P("frame", "head"),
        check_vma=False,
    )
```

```python
import functools

import jax
import jax.numpy as jnp
import numpy as np
from jax import lax
from jax.experimental import pallas as pl
from jax.experimental.pallas import tpu as pltpu
from jax.sharding import PartitionSpec as P

D = 1536
HD = 96
HALF_HD = HD // 2
KW = 31
HALF = 15
EDGE = 16
ROWS = 512
WIDTH = 384
QUARTER = 96
PIECE = 48
PART = 128
PARTS = ROWS // PART
SHARE = PART // 2
LANES = 128
CHUNK = 128
CHUNKS = ROWS // CHUNK
HEADS_HERE = 4
RING = 8
GROUP = 4
WINDOW = 9
UNIT = 2 * HD
PADDED_UNIT = UNIT + 16
SCALE = HD ** (-0.5) * 1.4426950408889634
MESH = pl.DeviceIdType.MESH
F32 = jnp.float32
BF16 = jnp.bfloat16


def contract(lhs, rhs, lhs_dim, rhs_dim):
    return lax.dot_general(
        lhs, rhs, (((lhs_dim,), (rhs_dim,)), ((), ())), preferred_element_type=F32
    )


def place(frame_count):
    frame = lax.axis_index("frame")
    head = lax.axis_index("head")
    ring, spot = frame // RING, frame % RING
    half, slot = spot // GROUP, spot % GROUP
    pair, core = head // 2, head % 2
    groups = frame_count // GROUP

    def partner(index):
        return (RING * ring + GROUP * core + index, 2 * pair + half)

    def is_self(index):
        return jnp.logical_and(core == half, slot == index)

    def group_device(by):
        group = (2 * ring + core + by + groups) % groups
        return (RING * (group // 2) + spot, 2 * pair + group % 2)

    def head_device(pair_flip, core_flip):
        to_pair = 1 - pair if pair_flip else pair
        to_core = 1 - core if core_flip else core
        return (frame, 2 * to_pair + to_core)

    def frame_device(by):
        return ((frame + by + frame_count) % frame_count, head)

    def spot_device(by):
        return (RING * ring + (spot + by + RING) % RING, head)

    def other_device():
        return (2 * RING * (ring // 2) + RING * (1 - ring % 2) + spot, 2 * (1 - pair) + core)

    return (
        partner,
        is_self,
        group_device,
        head_device,
        frame_device,
        spot_device,
        other_device,
        half,
        slot,
        core,
    )


def remote(source, target, send_sem, recv_sem, device):
    return pltpu.make_async_remote_copy(
        src_ref=source,
        dst_ref=target,
        send_sem=send_sem,
        recv_sem=recv_sem,
        device_id=device,
        device_id_type=MESH,
    )


def norm_rows(block):
    wide = block.astype(F32)
    center = wide - jnp.mean(wide, axis=-1, keepdims=True)
    spread = jnp.mean(center * center, axis=-1, keepdims=True)
    return (center * lax.rsqrt(spread + 1e-05)).astype(BF16)


def kernel(
    frame_count,
    frames_hbm,
    glu_hbm,
    depth_hbm,
    scale_hbm,
    shift_hbm,
    point_hbm,
    qkv_hbm,
    weight_hbm,
    angle_hbm,
    out_ref,
    frames,
    glu,
    point_all,
    key_value_weight,
    query_weight,
    weight_ref,
    angle,
    taps_ref,
    scale_ref,
    shift_ref,
    edges,
    normed,
    gated,
    swished,
    swished_all,
    sums,
    terms,
    residual,
    residual_send,
    normed_again,
    rotation,
    kv_ref,
    q_ref,
    kv_all,
    keys,
    q_all,
    scores,
    far_scores,
    peaks,
    totals,
    mixed,
    gathered,
    near_send,
    near_recv,
    far_own,
    far_send,
    far_recv,
    load_sem,
    edge_send_sem,
    edge_recv_sem,
    weight_y_send_sem,
    weight_y_recv_sem,
    weight_x_send_sem,
    weight_x_recv_sem,
    weight_near_send_sem,
    weight_near_recv_sem,
    swished_send_sem,
    swished_recv_sem,
    normed_send_sem,
    normed_recv_sem,
    residual_send_sem,
    residual_recv_sem,
    kv_send_sem,
    kv_recv_sem,
    q_send_sem,
    q_recv_sem,
    relay_send_sem,
    relay_recv_sem,
    o_send_sem,
    o_recv_sem,
    near_send_sem,
    near_recv_sem,
    far_send_sem,
    far_recv_sem,
):
    (
        partner,
        is_self,
        group_device,
        head_device,
        frame_device,
        spot_device,
        other_device,
        half,
        slot,
        core,
    ) = place(frame_count)
    frame = lax.axis_index("frame")
    own_head = lax.axis_index("head")
    pair = own_head // 2
    near_head = 2 * pair + 1 - core
    far_head = 2 * (1 - pair) + core
    cross_head = 2 * (1 - pair) + 1 - core

    def columns_of(head):
        return pl.ds(pl.multiple_of(head * WIDTH, 128), WIDTH)

    colour = (frame // (2 * RING) + frame % RING) % 4
    quarters = [colour, (colour + 2) % 4, (colour + 3) % 4, (colour + 1) % 4]

    def point_rows(head, start, size):
        return point_all.at[pl.ds(pl.multiple_of(head * WIDTH + start, 16), size)]

    loads = [
        pltpu.make_async_copy(point_hbm, point_rows(own_head, 0, WIDTH), load_sem.at[0]),
        pltpu.make_async_copy(frames_hbm, frames, load_sem.at[1]),
        pltpu.make_async_copy(glu_hbm.at[0], glu.at[:, pl.ds(0, WIDTH)], load_sem.at[2]),
        pltpu.make_async_copy(glu_hbm.at[1], glu.at[:, pl.ds(WIDTH, WIDTH)], load_sem.at[3]),
        pltpu.make_async_copy(depth_hbm, taps_ref, load_sem.at[4]),
        pltpu.make_async_copy(scale_hbm, scale_ref.at[0], load_sem.at[5]),
        pltpu.make_async_copy(shift_hbm, shift_ref.at[0], load_sem.at[6]),
        pltpu.make_async_copy(angle_hbm, angle, load_sem.at[7]),
        pltpu.make_async_copy(
            qkv_hbm.at[1], key_value_weight.at[:, pl.ds(0, WIDTH)], load_sem.at[8]
        ),
        pltpu.make_async_copy(
            qkv_hbm.at[2], key_value_weight.at[:, pl.ds(WIDTH, WIDTH)], load_sem.at[9]
        ),
        pltpu.make_async_copy(qkv_hbm.at[0], query_weight, load_sem.at[10]),
        pltpu.make_async_copy(weight_hbm, weight_ref, load_sem.at[11]),
    ]
    for load in loads[:7]:
        load.start()

    barrier = pltpu.get_barrier_semaphore()

    def greet(device):
        pl.semaphore_signal(barrier, inc=1, device_id=device, device_id_type=MESH)

    for index in range(GROUP):

        @pl.when(jnp.logical_not(is_self(index)))
        def _():
            greet(partner(index))

    greet(group_device(1))
    greet(group_device(-1))
    greet(head_device(False, True))
    greet(head_device(True, False))
    greet(head_device(True, True))
    greet(frame_device(1))
    greet(frame_device(-1))
    greet(frame_device(2 * RING))
    greet(frame_device(-2 * RING))
    greet(other_device())
    greet(spot_device(1))
    greet(spot_device(-1))
    pl.semaphore_wait(barrier, 16 - (core == half).astype(jnp.int32))

    def weight_y_copy(turn, side):
        block = point_rows(own_head, QUARTER * quarters[turn] + PIECE * side, PIECE)
        return remote(
            block,
            block,
            weight_y_send_sem.at[turn, side],
            weight_y_recv_sem.at[turn, side],
            other_device() if side else head_device(True, False),
        )

    def weight_y_arrival(turn, side):
        block = point_rows(far_head, QUARTER * quarters[turn] + PIECE * side, PIECE)
        return remote(
            block,
            block,
            weight_y_send_sem.at[turn, side],
            weight_y_recv_sem.at[turn, side],
            other_device() if side else head_device(True, False),
        )

    def weight_x_copy(way, side):
        block = point_rows(far_head, QUARTER * quarters[0] + PIECE * side, PIECE)
        return remote(
            block,
            block,
            weight_x_send_sem.at[way, side],
            weight_x_recv_sem.at[way, side],
            spot_device(-1 if way else 1) if side else frame_device(-2 * RING if way else 2 * RING),
        )

    def weight_x_arrival(way, side):
        block = point_rows(far_head, QUARTER * quarters[2 + way] + PIECE * side, PIECE)
        return remote(
            block,
            block,
            weight_x_send_sem.at[way, side],
            weight_x_recv_sem.at[way, side],
            spot_device(-1 if way else 1) if side else frame_device(-2 * RING if way else 2 * RING),
        )

    def weight_near_copy(index, arriving):
        if index == 0:
            block = point_rows(near_head if arriving else own_head, 0, WIDTH)
        else:
            block = point_rows(
                cross_head if arriving else far_head, QUARTER * quarters[index - 1], QUARTER
            )
        return remote(
            block,
            block,
            weight_near_send_sem.at[index],
            weight_near_recv_sem.at[index],
            head_device(False, True),
        )

    loads[0].wait()
    weight_y_copy(0, 0).start()
    weight_y_copy(0, 1).start()
    loads[1].wait()

    def edge_copy(side):
        rows = pl.ds(ROWS - EDGE, EDGE) if side == 0 else pl.ds(0, EDGE)
        return remote(
            frames.at[rows],
            edges.at[side],
            edge_send_sem.at[side],
            edge_recv_sem.at[side],
            frame_device(1 if side == 0 else -1),
        )

    edge_copy(0).start()
    edge_copy(1).start()

    def norm_block(index, carry):
        start = pl.multiple_of(index * 64, 64)
        normed[pl.ds(pl.multiple_of(start + EDGE, 16), 64)] = norm_rows(frames[pl.ds(start, 64)])
        return carry

    lax.fori_loop(0, ROWS // 64, norm_block, 0)
    weight_y_copy(1, 0).start()
    weight_y_copy(1, 1).start()
    weight_near_copy(0, False).start()
    for load in loads[7:]:
        load.start()
    edge_copy(0).wait_recv()
    normed[:EDGE] = norm_rows(edges[0])
    edge_copy(1).wait_recv()
    normed[ROWS + EDGE :] = norm_rows(edges[1])

    loads[2].wait()
    loads[3].wait()
    both = jnp.dot(normed[...], glu[...], preferred_element_type=F32)
    gated[...] = (both[:, :WIDTH] * jax.nn.sigmoid(both[:, WIDTH:])).astype(BF16).astype(F32)

    for side in range(2):
        weight_y_arrival(0, side).wait_recv()
        weight_x_copy(0, side).start()
        weight_x_copy(1, side).start()
    weight_near_copy(1, False).start()

    @pl.when(frame == 0)
    def _():
        gated[:EDGE] = jnp.zeros((EDGE, WIDTH), F32)

    @pl.when(frame == frame_count - 1)
    def _():
        gated[ROWS + EDGE :] = jnp.zeros((EDGE, WIDTH), F32)

    for load in loads[4:7]:
        load.wait()

    def share_rows(part, which):
        return pl.ds(pl.multiple_of(part * PART + SHARE * which, SHARE), SHARE)

    def swished_copy(part, index):
        flips = ((False, True), (True, False), (True, True))[index]
        return remote(
            swished.at[share_rows(part, core if index == 1 else 1 - core)],
            swished_all.at[part, own_head],
            swished_send_sem.at[part, index],
            swished_recv_sem.at[part, index],
            head_device(*flips),
        )

    def swished_arrival(part, index):
        head = (near_head, far_head, cross_head)[index]
        return remote(
            swished.at[share_rows(part, core)],
            swished_all.at[part, head],
            swished_send_sem.at[part, index],
            swished_recv_sem.at[part, index],
            head_device(False, True),
        )

    def normed_copy(part, arriving):
        block = normed_again.at[share_rows(part, 1 - core if arriving else core)]
        return remote(
            block,
            block,
            normed_send_sem.at[part],
            normed_recv_sem.at[part],
            head_device(False, True),
        )

    def residual_copy(part, arriving):
        return remote(
            residual_send.at[part],
            residual.at[share_rows(part, 1 - core if arriving else core)],
            residual_send_sem.at[part],
            residual_recv_sem.at[part],
            head_device(False, True),
        )

    def convolve(part):
        def piece(index, carry):
            lanes = pl.ds(pl.multiple_of(index * LANES, LANES), LANES)
            start = part * PART
            block = gated[pl.ds(start, PART + 2 * EDGE), lanes]
            taps = taps_ref[:, lanes]
            total = jnp.zeros((PART, LANES), F32)
            for shift in range(8):
                partial = jnp.zeros((PART + 8, LANES), F32)
                for step in range(4):
                    tap = 8 * step + shift - 1
                    if 0 <= tap < KW:
                        partial += taps[tap : tap + 1] * block[8 * step : 8 * step + PART + 8]
                total += partial[shift : shift + PART]
            shifted = total * scale_ref[:, lanes] + shift_ref[:, lanes]
            swished[pl.ds(start, PART), lanes] = (shifted * jax.nn.sigmoid(shifted)).astype(BF16)
            return carry

        lax.fori_loop(0, WIDTH // LANES, piece, 0)
        for index in (1, 2, 0):
            swished_copy(part, index).start()
        swished_all[part, own_head] = swished[share_rows(part, core)]

    def add_residual(part):
        for index in range(3):
            swished_arrival(part, index).wait_recv()
        rows = share_rows(part, core)
        whole = jnp.concatenate([swished_all[part, head] for head in range(4)], axis=1)
        sums[...] = frames[rows].astype(F32) + jnp.dot(
            whole, point_all[...], preferred_element_type=F32
        )
        normed_again[rows] = norm_rows(sums[...])
        normed_copy(part, False).start()
        residual[rows] = sums[:, columns_of(own_head)]
        residual_send[part] = sums[:, columns_of(near_head)]
        residual_copy(part, False).start()

    def kv_copy(part, index):
        return remote(
            kv_ref.at[part, index],
            kv_all.at[GROUP + slot, part, pl.ds(0, UNIT)],
            kv_send_sem.at[part, index],
            kv_recv_sem.at[part, slot],
            partner(index),
        )

    def kv_arrival(part, index):
        return remote(
            kv_ref.at[part, index],
            kv_all.at[GROUP + index, part, pl.ds(0, UNIT)],
            kv_send_sem.at[part, index],
            kv_recv_sem.at[part, index],
            partner(index),
        )

    def project(part):
        normed_copy(part, True).wait_recv()
        columns = pl.ds(part * PART, PART)
        turned = jnp.dot(
            normed_again[pl.ds(part * PART, PART)],
            key_value_weight[...],
            preferred_element_type=F32,
        ).T
        cosine, sine = rotation[0, :, columns], rotation[1, :, columns]
        for index in range(HEADS_HERE):
            base = index * HD
            first = turned[base : base + HALF_HD]
            second = turned[base + HALF_HD : base + HD]
            kv_ref[part, index, :HALF_HD] = (first * cosine - second * sine).astype(BF16)
            kv_ref[part, index, HALF_HD:HD] = (second * cosine + first * sine).astype(BF16)
            kv_ref[part, index, HD:] = turned[WIDTH + base : WIDTH + base + HD].astype(BF16)

    def send_pairs(part):
        for index in range(GROUP):

            @pl.when(jnp.logical_not(is_self(index)))
            def _():
                kv_copy(part, index).start()

            @pl.when(is_self(index))
            def _():
                kv_all[GROUP + slot, part, :UNIT] = kv_ref[part, index]

    def await_sent(copy, part):
        for index in range(GROUP):

            @pl.when(jnp.logical_not(is_self(index)))
            def _():
                copy(part, index).wait_send()

    for part in range(PARTS):
        convolve(part)

    for side in range(2):
        weight_y_arrival(1, side).wait_recv()
    weight_near_copy(2, False).start()
    for way in range(2):
        for side in range(2):
            weight_x_arrival(way, side).wait_recv()
        weight_near_copy(3 + way, False).start()

    loads[7].wait()
    lane = lax.broadcasted_iota(jnp.int32, (2, HALF_HD, LANES), 2)
    far = jnp.sum(
        jnp.where(lane == frame, angle[:, :, ROWS:], 0.0), axis=-1, keepdims=True
    )
    cosine, sine = angle[0, :, :ROWS], angle[1, :, :ROWS]
    rotation[0] = cosine * far[0] - sine * far[1]
    rotation[1] = sine * far[0] + cosine * far[1]
    for block in range(3 * GROUP):
        kv_all[block, :, UNIT:] = jnp.ones((PARTS, PADDED_UNIT - UNIT, PART), BF16)
    for load in loads[8:]:
        load.wait()

    for index in range(5):
        weight_near_copy(index, True).wait_recv()
    add_residual(0)
    for part in range(1, PARTS):
        add_residual(part)
        project(part - 1)
        if part <= 2:
            send_pairs(part - 1)
    project(PARTS - 1)

    turned_queries = (
        jnp.dot(normed_again[...], query_weight[...], preferred_element_type=F32) * SCALE
    ).T
    for index in range(HEADS_HERE):
        base = index * HD
        first = turned_queries[base : base + HALF_HD]
        second = turned_queries[base + HALF_HD : base + HD]
        cosine, sine = rotation[0], rotation[1]
        low = (first * cosine - second * sine).astype(BF16)
        high = (second * cosine + first * sine).astype(BF16)
        for chunk in range(CHUNKS):
            columns = slice(chunk * CHUNK, (chunk + 1) * CHUNK)
            q_ref[chunk, index, :HALF_HD] = low[:, columns]
            q_ref[chunk, index, HALF_HD:] = high[:, columns]

    def q_copy(chunk, index):
        return remote(
            q_ref.at[chunk, index],
            q_all.at[chunk, slot],
            q_send_sem.at[chunk, index],
            q_recv_sem.at[chunk, slot],
            partner(index),
        )

    def send_queries(chunk):
        for index in range(GROUP):

            @pl.when(jnp.logical_not(is_self(index)))
            def _():
                q_copy(chunk, index).start()

            @pl.when(is_self(index))
            def _():
                q_all[chunk, slot] = q_ref[chunk, index]

    def turn_keys(block, part):
        keys[block, pl.ds(part * PART, PART)] = kv_all[block, part, :HD].T

    def relay(part, index, upward):
        at = index if upward else 2 * GROUP + index
        flag = index if upward else GROUP + index
        return remote(
            kv_all.at[GROUP + index, part, pl.ds(0, UNIT)],
            kv_all.at[at, part, pl.ds(0, UNIT)],
            relay_send_sem.at[part, flag],
            relay_recv_sem.at[part, flag],
            group_device(1 if upward else -1),
        )

    for part in range(PARTS):
        await_sent(kv_copy, part)
        if part + 2 < PARTS:
            send_pairs(part + 2)
        else:
            send_queries(part + 2 - PARTS)
        for index in range(GROUP):

            @pl.when(jnp.logical_not(is_self(index)))
            def _():
                kv_arrival(part, index).wait_recv()

            relay(part, index, True).start()
            relay(part, index, False).start()
            turn_keys(GROUP + index, part)

    def relay_arrivals(near):
        low = core == (1 if near else 0)
        for part in range(PARTS):
            for index in range(GROUP):
                at = jnp.where(low, index, 2 * GROUP + index)
                flag = jnp.where(low, index, GROUP + index)
                remote(
                    kv_all.at[GROUP + index, part, pl.ds(0, UNIT)],
                    kv_all.at[at, part, pl.ds(0, UNIT)],
                    relay_send_sem.at[part, flag],
                    relay_recv_sem.at[part, flag],
                    group_device(1),
                ).wait_recv()
                turn_keys(at, part)

    relay_arrivals(True)

    def await_queries(chunk):
        for index in range(GROUP):

            @pl.when(jnp.logical_not(is_self(index)))
            def _():
                remote(
                    q_ref.at[chunk, index],
                    q_all.at[chunk, index],
                    q_send_sem.at[chunk, index],
                    q_recv_sem.at[chunk, index],
                    partner(index),
                ).wait_recv()

    def query_block(turn):
        return jnp.where(core == 1, turn, GROUP - 1 - turn)

    def key_block(turn, index):
        return jnp.where(core == 1, turn + index, 3 * GROUP - 1 - turn - index)

    def score(chunk, turn, first, last, target, buffer):
        turned = q_all[chunk, query_block(turn)]
        for index in range(first, last):
            target[buffer, index - first] = contract(
                keys[key_block(turn, index)], turned, 1, 0
            )

    def weigh(turn, first, last, source, buffer, largest, total):
        for index in range(first, last):
            weights = jnp.exp2(source[buffer, index - first] - largest).astype(BF16)
            block = key_block(turn, index)
            values = jnp.concatenate(
                [kv_all[block, part, HD:] for part in range(PARTS)], axis=1
            )
            total += contract(values, weights, 1, 0)
        return total

    def highest(source, buffer, count):
        return functools.reduce(
            jnp.maximum,
            [jnp.max(source[buffer, index], axis=0, keepdims=True) for index in range(count)],
        )

    def near_turn(chunk, turn, buffer):
        count = WINDOW - 1 - turn
        largest = highest(scores, buffer, count)
        peaks[chunk, turn, 0:1] = largest
        totals[chunk, turn] = weigh(
            turn, 0, count, scores, buffer, largest, jnp.zeros((HD + 16, CHUNK), F32)
        )

    def near_stage(chunk):
        score(chunk, 0, 0, WINDOW - 1, scores, 0)
        for turn in range(GROUP):
            if turn < GROUP - 1:
                score(chunk, turn + 1, 0, WINDOW - 2 - turn, scores, (turn + 1) % 2)
            near_turn(chunk, turn, turn % 2)

    def far_turn(chunk, turn, buffer):
        earlier = peaks[chunk, turn, 0:1]
        largest = jnp.maximum(earlier, highest(far_scores, buffer, turn + 1))
        total = weigh(
            turn,
            WINDOW - 1 - turn,
            WINDOW,
            far_scores,
            buffer,
            largest,
            totals[chunk, turn] * jnp.exp2(earlier - largest),
        )
        mixed[chunk, turn] = (total[:HD] / total[HD : HD + 1]).astype(BF16)

    def far_stage(chunk):
        score(chunk, 0, WINDOW - 1, WINDOW, far_scores, 0)
        for turn in range(GROUP):
            if turn < GROUP - 1:
                score(chunk, turn + 1, WINDOW - 2 - turn, WINDOW, far_scores, (turn + 1) % 2)
            far_turn(chunk, turn, turn % 2)

    def whole_turn(chunk, turn):
        if turn < GROUP - 1:
            score(chunk, turn + 1, 0, WINDOW, scores, (turn + 1) % 2)
        buffer = turn % 2
        total = weigh(
            turn,
            0,
            WINDOW,
            scores,
            buffer,
            highest(scores, buffer, WINDOW),
            jnp.zeros((HD + 16, CHUNK), F32),
        )
        mixed[chunk, turn] = (total[:HD] / total[HD : HD + 1]).astype(BF16)

    def o_copy(chunk, turn):
        return remote(
            mixed.at[chunk, turn],
            gathered.at[chunk, slot],
            o_send_sem.at[chunk, turn],
            o_recv_sem.at[chunk, slot],
            partner(query_block(turn)),
        )

    def send_mixed(chunk, turns):
        for turn in turns:

            @pl.when(is_self(query_block(turn)))
            def _():
                gathered[chunk, slot] = mixed[chunk, turn]

            @pl.when(jnp.logical_not(is_self(query_block(turn))))
            def _():
                o_copy(chunk, turn).start()

    def near_copy(chunk):
        return remote(
            near_send.at[chunk],
            near_recv.at[chunk],
            near_send_sem.at[chunk],
            near_recv_sem.at[chunk],
            head_device(False, True),
        )

    def far_copy(chunk):
        return remote(
            far_send.at[chunk],
            far_recv.at[chunk],
            far_send_sem.at[chunk],
            far_recv_sem.at[chunk],
            head_device(True, False),
        )

    def rows_of(chunk):
        return pl.ds(pl.multiple_of(chunk * CHUNK, CHUNK), CHUNK)

    def project_out(chunk):
        for index in range(GROUP):

            @pl.when(jnp.logical_not(is_self(index)))
            def _():
                remote(
                    mixed.at[chunk, index],
                    gathered.at[chunk, index],
                    o_send_sem.at[chunk, index],
                    o_recv_sem.at[chunk, index],
                    partner(index),
                ).wait_recv()

        turned = gathered[chunk].reshape(WIDTH, CHUNK).T
        terms[...] = jnp.dot(turned, weight_ref[...], preferred_element_type=F32)
        near_send[chunk, 0] = terms[:, columns_of(near_head)].astype(BF16)
        near_send[chunk, 1] = terms[:, columns_of(cross_head)].astype(BF16)
        near_copy(chunk).start()
        residual[rows_of(chunk)] += terms[:, columns_of(own_head)]
        far_own[chunk] = terms[:, columns_of(far_head)]

    def sum_out(chunk):
        near_copy(chunk).wait_recv()
        far_send[chunk] = (far_own[chunk] + near_recv[chunk, 1].astype(F32)).astype(BF16)
        far_copy(chunk).start()
        residual[rows_of(chunk)] += near_recv[chunk, 0].astype(F32)

    for part in range(PARTS):
        residual_copy(part, True).wait_recv()
    def early(chunk, carry):
        await_sent(q_copy, chunk)
        send_queries(chunk + 2)
        await_queries(chunk)
        near_stage(chunk)
        return carry

    lax.fori_loop(0, 2, early, 0)
    relay_arrivals(False)

    def finish(chunk, carry):
        far_stage(chunk)
        send_mixed(chunk, range(GROUP))
        return carry

    lax.fori_loop(0, 2, finish, 0)

    def late(chunk, carry):
        await_queries(chunk)
        score(chunk, 0, 0, WINDOW, scores, 0)
        whole_turn(chunk, 0)
        whole_turn(chunk, 1)
        send_mixed(chunk, (0, 1))
        project_out(chunk - 2)
        whole_turn(chunk, 2)
        whole_turn(chunk, 3)
        send_mixed(chunk, (2, 3))
        sum_out(chunk - 2)
        return carry

    lax.fori_loop(2, CHUNKS, late, 0)
    for chunk in range(2, CHUNKS):
        project_out(chunk)
        sum_out(chunk)
    def finish_rows(chunk):
        far_copy(chunk).wait_recv()
        rows = pl.ds(chunk * CHUNK, CHUNK)
        out_ref[rows] = (residual[rows] + far_recv[chunk].astype(F32)).astype(BF16)

    for chunk in range(CHUNKS - 2):
        finish_rows(chunk)

    for index in range(GROUP):

        @pl.when(jnp.logical_not(is_self(index)))
        def _():
            for chunk in range(2, CHUNKS):
                q_copy(chunk, index).wait_send()

        for part in range(PARTS):
            relay(part, index, True).wait_send()
            relay(part, index, False).wait_send()
    for turn in range(GROUP):

        @pl.when(jnp.logical_not(is_self(query_block(turn))))
        def _():
            for chunk in range(CHUNKS):
                o_copy(chunk, turn).wait_send()

    edge_copy(0).wait_send()
    edge_copy(1).wait_send()
    for part in range(PARTS):
        normed_copy(part, False).wait_send()
        residual_copy(part, False).wait_send()
        for index in range(3):
            swished_copy(part, index).wait_send()
    for side in range(2):
        for turn in range(2):
            weight_y_copy(turn, side).wait_send()
            weight_x_copy(turn, side).wait_send()
    for index in range(5):
        weight_near_copy(index, False).wait_send()
    for chunk in range(CHUNKS - 2, CHUNKS):
        finish_rows(chunk)
    for chunk in range(CHUNKS):
        near_copy(chunk).wait_send()
        far_copy(chunk).wait_send()


def angle_table(frame_count):
    inverse = 10000.0 ** (-np.arange(HALF_HD) * (2.0 / HD))
    starts = np.zeros(LANES)
    starts[:frame_count] = np.arange(frame_count) * float(ROWS)
    angles = inverse[:, None] * np.concatenate([np.arange(ROWS), starts])[None, :]
    return jnp.asarray(np.stack([np.cos(angles), np.sin(angles)]).astype(np.float32))


def shards(
    frame_count,
    frames,
    glu_weight,
    depth_kernel,
    bn_scale,
    bn_shift,
    point_weight,
    qkv_weight,
    out_weight,
):
    vmem = pl.BlockSpec(memory_space=pltpu.VMEM)
    hbm = pl.BlockSpec(memory_space=pl.ANY)
    dma = pltpu.SemaphoreType.DMA
    space = pltpu.VMEM
    return pl.pallas_call(
        functools.partial(kernel, frame_count),
        out_shape=jax.ShapeDtypeStruct((ROWS, WIDTH), BF16),
        in_specs=[hbm] * 9,
        out_specs=vmem,
        scratch_shapes=[
            space((ROWS, D), BF16),
            space((D, 2 * WIDTH), BF16),
            space((D, D), BF16),
            space((D, 2 * WIDTH), BF16),
            space((D, WIDTH), BF16),
            space((WIDTH, D), BF16),
            space((2, HALF_HD, ROWS + LANES), F32),
            space((KW, WIDTH), F32),
            space((1, WIDTH), F32),
            space((1, WIDTH), F32),
            space((2, EDGE, D), BF16),
            space((ROWS + 2 * EDGE, D), BF16),
            space((ROWS + 2 * EDGE, WIDTH), F32),
            space((ROWS, WIDTH), BF16),
            space((PARTS, 4, SHARE, WIDTH), BF16),
            space((SHARE, D), F32),
            space((CHUNK, D), F32),
            space((ROWS, WIDTH), F32),
            space((PARTS, SHARE, WIDTH), F32),
            space((ROWS, D), BF16),
            space((2, HALF_HD, ROWS), F32),
            space((PARTS, GROUP, UNIT, PART), BF16),
            space((CHUNKS, GROUP, HD, CHUNK), BF16),
            space((3 * GROUP, PARTS, PADDED_UNIT, PART), BF16),
            space((3 * GROUP, ROWS, HD), BF16),
            space((CHUNKS, GROUP, HD, CHUNK), BF16),
            space((2, WINDOW, ROWS, CHUNK), F32),
            space((2, GROUP, ROWS, CHUNK), F32),
            space((CHUNKS, GROUP, 8, CHUNK), F32),
            space((CHUNKS, GROUP, HD + 16, CHUNK), F32),
            space((CHUNKS, GROUP, HD, CHUNK), BF16),
            space((CHUNKS, GROUP, HD, CHUNK), BF16),
            space((CHUNKS, 2, CHUNK, WIDTH), BF16),
            space((CHUNKS, 2, CHUNK, WIDTH), BF16),
            space((CHUNKS, CHUNK, WIDTH), F32),
            space((CHUNKS, CHUNK, WIDTH), BF16),
            space((CHUNKS, CHUNK, WIDTH), BF16),
            dma((12,)),
            dma((2,)),
            dma((2,)),
            dma((2, 2)),
            dma((2, 2)),
            dma((2, 2)),
            dma((2, 2)),
            dma((5,)),
            dma((5,)),
            dma((PARTS, 3)),
            dma((PARTS, 3)),
            dma((PARTS,)),
            dma((PARTS,)),
            dma((PARTS,)),
            dma((PARTS,)),
            dma((PARTS, GROUP)),
            dma((PARTS, GROUP)),
            dma((CHUNKS, GROUP)),
            dma((CHUNKS, GROUP)),
            dma((PARTS, 2 * GROUP)),
            dma((PARTS, 2 * GROUP)),
            dma((CHUNKS, GROUP)),
            dma((CHUNKS, GROUP)),
            dma((CHUNKS,)),
            dma((CHUNKS,)),
            dma((CHUNKS,)),
            dma((CHUNKS,)),
        ],
        compiler_params=pltpu.CompilerParams(
            collective_id=1, has_side_effects=True, vmem_limit_bytes=60 << 20
        ),
    )(
        frames,
        glu_weight,
        depth_kernel,
        bn_scale,
        bn_shift,
        point_weight,
        qkv_weight,
        out_weight,
        angle_table(frame_count),
    )


def solution(mesh):
    return jax.shard_map(
        functools.partial(shards, mesh.shape["frame"]),
        mesh=mesh,
        in_specs=(
            P("frame", None),
            P(None, None, "head"),
            P(None, "head"),
            P("head"),
            P("head"),
            P("head", None),
            P(None, None, "head"),
            P("head", None),
        ),
        out_specs=P("frame", "head"),
        check_vma=False,
    )
```
